512 devices in a mesh: replica: 8 (over z_lo), fsdp: 64 (over y, x, z_hi, core).
Axes of the slice: x: 4, y: 4, z: 16 (z_hi: 2, z_lo: 8; z = z_hi * 8 + z_lo), core: 2. Of those that a mesh axis runs over, the one named last changes fastest.
Arguments:
- activations: bfloat16 [8, 8192, 6144], P('replica', 'fsdp'), may hold values from -0.0625 to 0.0625
- up_cotangent: bfloat16 [8, 8192, 512], P('replica', 'fsdp'), may hold values from -6 to 6
- up_weight: bfloat16 [8, 6144, 512], P('replica', 'fsdp'), may hold values from -0.25 to 0.25
- pseudo_grads: bfloat16 [8, 6144, 384], P('replica', 'fsdp'), may hold values from -6 to 6
- outer_params: float32 [6144, 384], P('fsdp'), may hold values from -6 to 6
- outer_moment: float32 [6144, 384], P('fsdp'), may hold values from -6 to 6
Outputs:
- grad_input: bfloat16 [8, 8192, 6144], P('replica', 'fsdp')
- grad_weight: float32 [8, 6144, 512], P('replica', 'fsdp')
- new_params: float32 [6144, 384], P('fsdp')
- new_moment: float32 [6144, 384], P('fsdp')
The draws below stay inside these ranges and needn't reach their ends.
All inputs are finite; a program needn't handle non-finite values.
Results may differ from the reference program's by a relative error of at most 0.008.
Values may be sent and summed in bfloat16 or wider, within the bound.
A program may use at most 64 MiB of HBM per device.

```python
import jax
import jax.numpy as jnp
from jax import lax

D = 6144
FW = 512
FRAG = 384
TOKENS = 8192
N_REPLICA = 8


def shard_levels(rng, dims, split, low, largest):
    factor_of = 1.0
    for dim, parts in split:
        heights = jax.random.uniform(jax.random.fold_in(jax.random.fold_in(rng, 6), dim), (parts,), jnp.float32, low / len(split), largest / len(split))
        factor_of = factor_of * jnp.repeat(jnp.exp(heights), dims[dim] // parts).reshape((-1,) + (1,) * (len(dims) - 1 - dim))
    return factor_of


def gaussian(rng, dims, deviation, reach, split=(), kind=jnp.bfloat16):
    factor_of = shard_levels(rng, dims, split, -0.22, 0.18) if split else 1.0
    values = jax.random.normal(rng, dims, jnp.float32) * deviation * factor_of
    return jnp.minimum(jnp.maximum(values, -reach), reach).astype(kind)


def setup_inputs(seed: int = 0) -> dict:
    splits = jax.random.split(jax.random.key(seed), 7)
    return {
        "activations": gaussian(splits[0], (N_REPLICA, TOKENS, D), TOKENS ** -0.5, 0.0625, ((0, 8), (1, 64))),
        "up_cotangent": gaussian(splits[1], (N_REPLICA, TOKENS, FW), 1.0, 6.0, ((0, 8), (1, 64))),
        "up_weight": gaussian(splits[2], (N_REPLICA, D, FW), FW ** -0.5, 0.25, ((0, 8), (1, 64))),
        "pseudo_grads": gaussian(splits[3], (N_REPLICA, D, FRAG), 1.0, 6.0, ((0, 8), (1, 64))),
        "outer_params": gaussian(splits[4], (D, FRAG), 1.0, 6.0, ((0, 64),), jnp.float32),
        "outer_moment": gaussian(splits[5], (D, FRAG), 1.0, 6.0, ((0, 64),), jnp.float32),
    }


outer_rate = 0.7
outer_beta = 0.9


def reference(activations, up_cotangent, up_weight, pseudo_grads, outer_params, outer_moment):
    inputs_list = []
    weights_list = []
    for group in range(N_REPLICA):
        inputs_list.append(jnp.dot(up_cotangent[group], up_weight[group].T, preferred_element_type=jnp.float32).astype(jnp.bfloat16))
        weights_list.append(lax.dot_general(activations[group], up_cotangent[group], (((0,), (0,)), ((), ())), preferred_element_type=jnp.float32))
    grad_input = jnp.stack(inputs_list)
    grad_weight = jnp.stack(weights_list)
    average = jnp.sum(pseudo_grads.astype(jnp.float32), axis=0) / N_REPLICA
    new_moment = outer_beta * outer_moment + average
    new_params = outer_params - outer_rate * (average + outer_beta * new_moment)
    return grad_input, grad_weight, new_params, new_moment
```

```python
import jax
import jax.numpy as jnp
from jax import lax
from jax.experimental import pallas as pl
from jax.experimental.pallas import tpu as pltpu
from jax.sharding import PartitionSpec as P

outer_rate = 0.7
outer_beta = 0.9

SIDE = 4
GROUPS = 8
TOK = 128
ROWS = 96
D = 6144
FW = 512
HALF = FW // 2
PART = HALF // 2
BLOCK = 4 * ROWS
FRAG = 384
CUT = ROWS // GROUPS
PAD = 16
HROWS = ROWS // 2

MESH = pl.DeviceIdType.MESH
ORDER = (1, 3, 2)


def kernel(
    act, cot, weight, pseudo, params, moment,
    gi_out, gw_out, params_out, moment_out,
    a_buf, c_buf, ct_buf, p_x, p_y, r_x, r_y, s_x, s_y, q_x, q_y, total, z_src, z_dst, swap, gw_buf,
    w_buf, gi_buf, g_buf, g_wide, g_src, g_dst, h_src, h_dst, par_buf, mom_buf,
    load_sem, store_sem, core_send, core_recv, rs_send, rs_recv, z_send, z_recv,
    w1_send, w1_recv, w2_send, w2_recv, wc_send, wc_recv, g_send, g_recv, h_send, h_recv,
):
    r = lax.axis_index("replica")
    f = lax.axis_index("fsdp")
    y, x, zh, c = f // 16, (f // 4) % 4, (f // 2) % 2, f % 2

    def at(y, x, zh, c):
        return (r, ((y * 4 + x) * 2 + zh) * 2 + c)

    def along_x(k):
        return at(y, (x + k) % 4, zh, c)

    def along_y(k):
        return at((y + k) % 4, x, zh, c)

    def along_r(k):
        return ((r + k) % GROUPS, f)

    peer = at(y, x, zh, 1 - c)
    across = at(y, x, 1 - zh, c)

    sent = []

    def send(src, dst, ss, rs, to):
        copy = pltpu.make_async_remote_copy(
            src_ref=src, dst_ref=dst, send_sem=ss, recv_sem=rs, device_id=to, device_id_type=MESH
        )
        copy.start()
        sent.append(copy)
        return copy

    own_w = w_buf.at[y, x, pl.ds(pl.multiple_of((zh * 2 + c) * ROWS, ROWS), ROWS)]
    loads = [
        pltpu.make_async_copy(weight, own_w, load_sem.at[0]),
        pltpu.make_async_copy(cot, c_buf.at[0], load_sem.at[1]),
        pltpu.make_async_copy(act, a_buf.at[pl.ds(0, TOK)], load_sem.at[2]),
        pltpu.make_async_copy(pseudo, g_buf, load_sem.at[3]),
        pltpu.make_async_copy(params, par_buf, load_sem.at[4]),
        pltpu.make_async_copy(moment, mom_buf, load_sem.at[5]),
    ]
    for copy in loads:
        copy.start()

    barrier = pltpu.get_barrier_semaphore()
    friends = [peer, across]
    friends += [along_x(k) for k in ORDER] + [along_y(k) for k in ORDER]
    friends += [along_r(k) for k in range(1, GROUPS)]
    for to in friends:
        pl.semaphore_signal(barrier, inc=1, device_id=to, device_id_type=MESH)

    loads[3].wait()
    g_wide[...] = g_buf[...].astype(jnp.float32)
    for j in range(GROUPS):
        g_src[j, 0:CUT, :] = g_wide[j * CUT:(j + 1) * CUT, :]
        g_src[j, CUT:PAD, :] = jnp.zeros((PAD - CUT, FRAG), jnp.float32)
    for j in range(GROUPS):
        h_src[j] = g_src[j].astype(jnp.bfloat16)
    loads[0].wait()
    loads[1].wait()
    loads[2].wait()
    pl.semaphore_wait(barrier, len(friends))

    z_w = send(own_w, own_w, z_send.at[0], z_recv.at[0], across)
    c_copy = send(c_buf.at[0], c_buf.at[1], core_send.at[0], core_recv.at[0], peer)
    a_copies = []
    for i, k in enumerate((1, 3, 2, 0)):
        cols = pl.ds(pl.multiple_of(((y + k) % 4) * (4 * BLOCK), 128), 4 * BLOCK)
        a_copies.append(
            send(
                a_buf.at[pl.ds(0, TOK), cols], a_buf.at[pl.ds(TOK, TOK), cols],
                core_send.at[1 + i], core_recv.at[1 + i], peer,
            )
        )

    def w_rows(plane, second):
        return pl.ds(pl.multiple_of((plane * 2 + c) * ROWS + second * HROWS, 16), HROWS)

    def w_first(s, plane):
        copies = []
        for k in ORDER:
            ref = w_buf.at[y, x, w_rows(plane, 0)]
            copies.append(send(ref, ref, w1_send.at[s, 0, k - 1], w1_recv.at[s, 0, k - 1], along_x(k)))
            ref = w_buf.at[y, x, w_rows(plane, 1)]
            copies.append(send(ref, ref, w1_send.at[s, 1, k - 1], w1_recv.at[s, 1, k - 1], along_y(k)))
        return copies

    def w_second(s, plane):
        copies = []
        for k in ORDER:
            ref = w_buf.at[y, :, w_rows(plane, 0)]
            copies.append(send(ref, ref, w2_send.at[s, 0, k - 1], w2_recv.at[s, 0, k - 1], along_y(k)))
            ref = w_buf.at[:, x, w_rows(plane, 1)]
            copies.append(send(ref, ref, w2_send.at[s, 1, k - 1], w2_recv.at[s, 1, k - 1], along_x(k)))
        return copies

    def w_core(s, plane, k):
        ref = w_buf.at[(y - k) % 4, :, w_rows(plane, 0)]
        one = send(ref, ref, wc_send.at[s, 0, k], wc_recv.at[s, 0, k], peer)
        ref = w_buf.at[:, (x - k) % 4, w_rows(plane, 1)]
        two = send(ref, ref, wc_send.at[s, 1, k], wc_recv.at[s, 1, k], peer)
        return [one, two]

    w1_own = w_first(0, zh)

    g_copies = []
    for k in range(1, GROUPS):
        g_copies.append(
            send(h_src.at[(r + k) % GROUPS], g_dst.at[k], g_send.at[k], g_recv.at[k], along_r(k))
        )

    c_copy.wait_recv()
    mine = pl.ds(pl.multiple_of(c * HALF, HALF), HALF)
    ct_buf[:, 0:TOK] = c_buf[0, :, mine].T
    ct_buf[:, TOK:2 * TOK] = c_buf[1, :, mine].T
    rs_copies_y = []
    for i, k in enumerate((1, 3, 2, 0)):
        a_copies[i].wait_recv()

        def block(j, _, k=k):
            col = pl.multiple_of((((y + k) % 4) * 4 + (x + j) % 4) * BLOCK, 128)
            part = jnp.dot(ct_buf[...], a_buf[:, pl.ds(col, BLOCK)], preferred_element_type=jnp.float32)
            part = part.astype(jnp.bfloat16)
            p_x[j, k] = part[0:PART]
            p_y[k, j] = part[PART:HALF]
            return 0

        lax.fori_loop(0, 4, block, 0)
        if k:
            rs_copies_y.append(
                send(p_y.at[k], r_y.at[k - 1], rs_send.at[0, 1, k - 1], rs_recv.at[0, 1, k - 1], along_y(k))
            )
    rs_copies_x = [
        send(p_x.at[k], r_x.at[k - 1], rs_send.at[0, 0, k - 1], rs_recv.at[0, 0, k - 1], along_x(k)) for k in ORDER
    ]

    for copy in g_copies:
        copy.wait_recv()
    cut = h_src[r].astype(jnp.float32)
    for k in range(1, GROUPS):
        cut = cut + g_dst[k].astype(jnp.float32)
    h_dst[r] = cut.astype(jnp.bfloat16)
    h_copies = [
        send(h_dst.at[r], h_dst.at[r], h_send.at[k], h_recv.at[k], along_r(k)) for k in range(1, GROUPS)
    ]

    z_w.wait_recv()
    w1_other = w_first(1, 1 - zh)

    for copy in rs_copies_x + rs_copies_y:
        copy.wait_recv()
    rs2 = []
    for k in ORDER:
        acc = p_x[0, k].astype(jnp.float32)
        for j in range(3):
            acc = acc + r_x[j, k].astype(jnp.float32)
        s_x[k - 1] = acc.astype(jnp.bfloat16)
        rs2.append(send(s_x.at[k - 1], q_x.at[k - 1], rs_send.at[1, 0, k - 1], rs_recv.at[1, 0, k - 1], along_y(k)))
        acc = p_y[0, k].astype(jnp.float32)
        for j in range(3):
            acc = acc + r_y[j, k].astype(jnp.float32)
        s_y[k - 1] = acc.astype(jnp.bfloat16)
        rs2.append(send(s_y.at[k - 1], q_y.at[k - 1], rs_send.at[1, 1, k - 1], rs_recv.at[1, 1, k - 1], along_x(k)))

    for copy in w1_own:
        copy.wait_recv()
    w2_own = w_second(0, zh)
    for copy in w1_other:
        copy.wait_recv()
    w2_other = w_second(1, 1 - zh)
    wc = w_core(0, zh, 0) + w_core(1, 1 - zh, 0)

    loads[4].wait()
    loads[5].wait()
    for copy in h_copies:
        copy.wait_recv()
    for j in range(GROUPS):
        g_wide[j * CUT:(j + 1) * CUT, :] = h_dst[j].astype(jnp.float32)[0:CUT]
    average = g_wide[...] / GROUPS
    new_moment = outer_beta * mom_buf[...] + average
    mom_buf[...] = new_moment
    par_buf[...] = par_buf[...] - outer_rate * (average + outer_beta * new_moment)
    stores = [
        pltpu.make_async_copy(par_buf, params_out, store_sem.at[0]),
        pltpu.make_async_copy(mom_buf, moment_out, store_sem.at[1]),
    ]
    for copy in stores:
        copy.start()

    for copy in rs2:
        copy.wait_recv()
    for i, (p, rr, q) in enumerate(((p_x, r_x, q_x), (p_y, r_y, q_y))):
        acc = p[0, 0].astype(jnp.float32)
        for j in range(3):
            acc = acc + rr[j, 0].astype(jnp.float32)
        for j in range(3):
            acc = acc + q[j].astype(jnp.float32)
        total[:, i * PART:(i + 1) * PART] = acc.T
    other = pl.ds(pl.multiple_of((1 - zh) * 2 * ROWS, 16), 2 * ROWS)
    z_src[...] = total[other, :].astype(jnp.bfloat16)
    z_g = send(z_src, z_dst, z_send.at[1], z_recv.at[1], across)

    for s, plane, copies in ((0, zh, w2_own), (1, 1 - zh, w2_other)):
        for i, k in enumerate(ORDER):
            copies[2 * i].wait_recv()
            copies[2 * i + 1].wait_recv()
            wc += w_core(s, plane, k)
    for copy in wc:
        copy.wait_recv()
    own_c = c_buf[0]

    def row(j, _):
        def col(i, _):
            blk = lax.dot_general(
                own_c, w_buf[j, i], (((1,), (1,)), ((), ())), preferred_element_type=jnp.float32
            )
            gi_buf[:, pl.ds(pl.multiple_of((j * 4 + i) * BLOCK, 128), BLOCK)] = blk.astype(jnp.bfloat16)
            return 0

        return lax.fori_loop(0, 4, col, 0)

    lax.fori_loop(0, 4, row, 0)
    gi_store = pltpu.make_async_copy(gi_buf, gi_out, store_sem.at[2])
    gi_store.start()

    z_g.wait_recv()
    first = pl.multiple_of(zh * 2 * ROWS, 16)
    theirs = pl.multiple_of((1 - c) * ROWS, 16)
    ours = pl.multiple_of(c * ROWS, 16)
    swap[...] = total[pl.ds(first + theirs, ROWS), :] + z_dst[pl.ds(theirs, ROWS), :].astype(jnp.float32)
    sw = send(swap, gw_buf.at[:, mine], core_send.at[5], core_recv.at[5], peer)
    gw_buf[:, mine] = total[pl.ds(first + ours, ROWS), :] + z_dst[pl.ds(ours, ROWS), :].astype(jnp.float32)
    sw.wait_recv()
    gw_store = pltpu.make_async_copy(gw_buf, gw_out, store_sem.at[3])
    gw_store.start()

    for copy in sent:
        copy.wait_send()
    for copy in stores:
        copy.wait()
    gi_store.wait()
    gw_store.wait()


def body(activations, up_cotangent, up_weight, pseudo_grads, outer_params, outer_moment):
    bf16, f32 = jnp.bfloat16, jnp.float32
    dma = pltpu.SemaphoreType.DMA
    any_space = pl.BlockSpec(memory_space=pl.ANY)
    gi, gw, new_params, new_moment = pl.pallas_call(
        kernel,
        out_shape=(
            jax.ShapeDtypeStruct((TOK, D), bf16),
            jax.ShapeDtypeStruct((ROWS, FW), f32),
            jax.ShapeDtypeStruct((ROWS, FRAG), f32),
            jax.ShapeDtypeStruct((ROWS, FRAG), f32),
        ),
        in_specs=[any_space] * 6,
        out_specs=(any_space,) * 4,
        scratch_shapes=[
            pltpu.VMEM((2 * TOK, D), bf16),
            pltpu.VMEM((2, TOK, FW), bf16),
            pltpu.VMEM((HALF, 2 * TOK), bf16),
            pltpu.VMEM((4, 4, PART, BLOCK), bf16),
            pltpu.VMEM((4, 4, PART, BLOCK), bf16),
            pltpu.VMEM((3, 4, PART, BLOCK), bf16),
            pltpu.VMEM((3, 4, PART, BLOCK), bf16),
            pltpu.VMEM((3, PART, BLOCK), bf16),
            pltpu.VMEM((3, PART, BLOCK), bf16),
            pltpu.VMEM((3, PART, BLOCK), bf16),
            pltpu.VMEM((3, PART, BLOCK), bf16),
            pltpu.VMEM((BLOCK, HALF), f32),
            pltpu.VMEM((2 * ROWS, HALF), bf16),
            pltpu.VMEM((2 * ROWS, HALF), bf16),
            pltpu.VMEM((ROWS, HALF), f32),
            pltpu.VMEM((ROWS, FW), f32),
            pltpu.VMEM((4, 4, BLOCK, FW), bf16),
            pltpu.VMEM((TOK, D), bf16),
            pltpu.VMEM((ROWS, FRAG), bf16),
            pltpu.VMEM((ROWS, FRAG), f32),
            pltpu.VMEM((GROUPS, PAD, FRAG), f32),
            pltpu.VMEM((GROUPS, PAD, FRAG), bf16),
            pltpu.VMEM((GROUPS, PAD, FRAG), bf16),
            pltpu.VMEM((GROUPS, PAD, FRAG), bf16),
            pltpu.VMEM((ROWS, FRAG), f32),
            pltpu.VMEM((ROWS, FRAG), f32),
            dma((6,)),
            dma((4,)),
            dma((6,)),
            dma((6,)),
            dma((2, 2, 3)),
            dma((2, 2, 3)),
            dma((2,)),
            dma((2,)),
            dma((2, 2, 3)),
            dma((2, 2, 3)),
            dma((2, 2, 3)),
            dma((2, 2, 3)),
            dma((2, 2, 4)),
            dma((2, 2, 4)),
            dma((GROUPS,)),
            dma((GROUPS,)),
            dma((GROUPS,)),
            dma((GROUPS,)),
        ],
        compiler_params=pltpu.CompilerParams(
            collective_id=0, has_side_effects=True, vmem_limit_bytes=62 * 1024 * 1024
        ),
        cost_estimate=pl.CostEstimate(flops=2 * 2 * TOK * D * FW, bytes_accessed=8 << 20, transcendentals=0),
        name="up_backward",
    )(
        activations[0], up_cotangent[0], up_weight[0], pseudo_grads[0], outer_params, outer_moment
    )
    return gi[None], gw[None], new_params, new_moment


def solution(mesh):
    placed = (
        P("replica", "fsdp", None),
        P("replica", "fsdp", None),
        P("replica", "fsdp", None),
        P("replica", "fsdp", None),
        P("fsdp", None),
        P("fsdp", None),
    )
    return jax.shard_map(
        body,
        mesh=mesh,
        in_specs=placed,
        out_specs=(
            P("replica", "fsdp", None),
            P("replica", "fsdp", None),
            P("fsdp", None),
            P("fsdp", None),
        ),
        check_vma=False,
    )
```

```python
import functools

import jax
import jax.numpy as jnp
from jax import lax
from jax.experimental import pallas as pl
from jax.experimental.pallas import tpu as pltpu
from jax.sharding import PartitionSpec as P

outer_rate = 0.7
outer_beta = 0.9

SIDE = 4
GROUPS = 8
TOK = 128
ROWS = 96
D = 6144
FW = 512
HALF = FW // 2
PART = HALF // 2
BLOCK = 4 * ROWS
FRAG = 384
CUT = ROWS // GROUPS
PAD = 16
HROWS = ROWS // 2

MESH = pl.DeviceIdType.MESH
ORDER = (1, 3, 2)
A_ORDER = [(j, 2) for j in range(4)] + [(2, k) for k in (0, 1, 3)]
A_ORDER += [(j, k) for j in (1, 3, 0) for k in (0, 1, 3)]


def kernel(
    act, cot, weight, pseudo, params, moment,
    gi_out, gw_out, params_out, moment_out,
    a_buf, c_buf, ct_buf, p_x, p_y, r_x, r_y, s_x, s_y, q_x, q_y, total, z_src, z_dst, swap,
    w_buf, g_buf, g_wide, g_src, g_dst, h_src, h_dst, par_buf, mom_buf,
    load_sem, core_send, core_recv, a_send, a_recv, rs_send, rs_recv, rs2_send, rs2_recv, z_send, z_recv,
    w1_send, w1_recv, w2_send, w2_recv, wc_send, wc_recv, g_send, g_recv, h_send, h_recv,
):
    r = lax.axis_index("replica")
    f = lax.axis_index("fsdp")
    y, x, zh, c = f // 16, (f // 4) % 4, (f // 2) % 2, f % 2

    def at(y, x, zh, c):
        return (r, ((y * 4 + x) * 2 + zh) * 2 + c)

    def along_x(k):
        return at(y, (x + k) % 4, zh, c)

    def along_y(k):
        return at((y + k) % 4, x, zh, c)

    def along_r(k):
        return ((r + k) % GROUPS, f)

    peer = at(y, x, zh, 1 - c)
    across = at(y, x, 1 - zh, c)

    sent = []

    def send(src, dst, ss, rs, to):
        copy = pltpu.make_async_remote_copy(
            src_ref=src, dst_ref=dst, send_sem=ss, recv_sem=rs, device_id=to, device_id_type=MESH
        )
        copy.start()
        sent.append(copy)
        return copy

    own_w = w_buf.at[y, x, pl.ds(pl.multiple_of((zh * 2 + c) * ROWS, ROWS), ROWS)]
    loads = [
        pltpu.make_async_copy(weight, own_w, load_sem.at[0]),
        pltpu.make_async_copy(cot, c_buf.at[0], load_sem.at[1]),
        pltpu.make_async_copy(act, a_buf.at[pl.ds(0, TOK)], load_sem.at[2]),
        pltpu.make_async_copy(pseudo, g_buf, load_sem.at[3]),
        pltpu.make_async_copy(params, par_buf, load_sem.at[4]),
        pltpu.make_async_copy(moment, mom_buf, load_sem.at[5]),
    ]
    for copy in loads:
        copy.start()

    barrier = pltpu.get_barrier_semaphore()
    friends = [peer, across]
    friends += [along_x(k) for k in ORDER] + [along_y(k) for k in ORDER]
    friends += [along_r(k) for k in range(1, GROUPS)]
    for to in friends:
        pl.semaphore_signal(barrier, inc=1, device_id=to, device_id_type=MESH)

    loads[3].wait()
    g_wide[...] = g_buf[...].astype(jnp.float32)
    for j in range(GROUPS):
        g_src[j, 0:CUT, :] = g_wide[j * CUT:(j + 1) * CUT, :]
        g_src[j, CUT:PAD, :] = jnp.zeros((PAD - CUT, FRAG), jnp.float32)
    for j in range(GROUPS):
        h_src[j] = g_src[j].astype(jnp.bfloat16)
    loads[0].wait()
    loads[1].wait()
    loads[2].wait()
    pl.semaphore_wait(barrier, len(friends))

    z_w = send(own_w, own_w, z_send.at[0], z_recv.at[0], across)
    c_copy = send(c_buf.at[0], c_buf.at[1], core_send.at[0], core_recv.at[0], peer)

    def a_cols(j, k):
        return pl.ds(pl.multiple_of((((y + k) % 4) * 4 + (x + j) % 4) * BLOCK, 128), BLOCK)

    def a_one(j, k):
        return pltpu.make_async_remote_copy(
            src_ref=a_buf.at[pl.ds(0, TOK), a_cols(j, k)], dst_ref=a_buf.at[pl.ds(TOK, TOK), a_cols(j, k)],
            send_sem=a_send.at[j, k], recv_sem=a_recv.at[j, k], device_id=peer, device_id_type=MESH,
        )

    for j, k in A_ORDER:
        a_one(j, k).start()

    def w_rows(plane, second):
        return pl.ds(pl.multiple_of((plane * 2 + c) * ROWS + second * HROWS, 16), HROWS)

    def w_first(s, plane):
        copies = []
        for k in ORDER:
            ref = w_buf.at[y, x, w_rows(plane, 0)]
            copies.append(send(ref, ref, w1_send.at[s, 0, k - 1], w1_recv.at[s, 0, k - 1], along_x(k)))
            ref = w_buf.at[y, x, w_rows(plane, 1)]
            copies.append(send(ref, ref, w1_send.at[s, 1, k - 1], w1_recv.at[s, 1, k - 1], along_y(k)))
        return copies

    def w_second(s, plane):
        copies = []
        for d, to in ((0, 1), (1, 3)):
            ref = w_buf.at[y, :, w_rows(plane, 0)]
            copies.append(send(ref, ref, w2_send.at[s, 0, 0, d], w2_recv.at[s, 0, 0, d], along_y(to)))
            ref = w_buf.at[:, x, w_rows(plane, 1)]
            copies.append(send(ref, ref, w2_send.at[s, 1, 0, d], w2_recv.at[s, 1, 0, d], along_x(to)))
        return copies

    def w_third(s, plane, copies):
        out, core = [], []
        for d, to in ((0, 1), (1, 3)):
            copies[2 * d].wait_recv()
            ref = w_buf.at[(y - to) % 4, pl.ds(2 * d, 2), w_rows(plane, 0)]
            out.append(send(ref, ref, w2_send.at[s, 0, 1, d], w2_recv.at[s, 0, 1, d], along_y(to)))
            copies[2 * d + 1].wait_recv()
            ref = w_buf.at[pl.ds(2 * d, 2), (x - to) % 4, w_rows(plane, 1)]
            out.append(send(ref, ref, w2_send.at[s, 1, 1, d], w2_recv.at[s, 1, 1, d], along_x(to)))
            core += w_core(s, plane, to)
        return out, core

    def w_core(s, plane, k):
        ref = w_buf.at[(y - k) % 4, :, w_rows(plane, 0)]
        one = send(ref, ref, wc_send.at[s, 0, k], wc_recv.at[s, 0, k], peer)
        ref = w_buf.at[:, (x - k) % 4, w_rows(plane, 1)]
        two = send(ref, ref, wc_send.at[s, 1, k], wc_recv.at[s, 1, k], peer)
        return [one, two]

    w1_own = w_first(0, zh)

    c_copy.wait_recv()
    mine = pl.ds(pl.multiple_of(c * HALF, HALF), HALF)
    ct_buf[:, 0:TOK] = c_buf[0, :, mine].T
    ct_buf[:, TOK:2 * TOK] = c_buf[1, :, mine].T

    def block(i, _, pick):
        j, k = pick(i)
        a_one(j, k).wait_recv()
        part = jnp.dot(ct_buf[...], a_buf[:, a_cols(j, k)], preferred_element_type=jnp.float32)
        part = part.astype(jnp.bfloat16)
        p_x[j, k] = part[0:PART]
        p_y[k, j] = part[PART:HALF]
        return 0

    def blocks(count, pick):
        lax.fori_loop(0, count, functools.partial(block, pick=pick), 0)

    axes = ((p_x, r_x, s_x, q_x, along_x, along_y), (p_y, r_y, s_y, q_y, along_y, along_x))

    def two_away(axis):
        p, rr, _, _, along, _ = axes[axis]
        return [
            send(p.at[2, pl.ds(2 * d, 2)], rr.at[0, d], rs_send.at[axis, 0, d], rs_recv.at[axis, 0, d], along(to))
            for d, to in ((0, 1), (1, 3))
        ]

    def plain(axis):
        p, rr, _, _, along, _ = axes[axis]
        return [
            send(p.at[to, pl.ds(2 - 2 * d, 2)], rr.at[1, d], rs_send.at[axis, 1, d], rs_recv.at[axis, 1, d], along(to))
            for d, to in ((0, 1), (1, 3))
        ]

    def added(axis, copies):
        p, rr, _, _, along, _ = axes[axis]
        out = []
        for d, to in ((0, 1), (1, 3)):
            copies[d].wait_recv()
            for j in range(2):
                acc = p[to, 2 * d + j].astype(jnp.float32) + rr[0, d, j].astype(jnp.float32)
                p[to, 2 * d + j] = acc.astype(jnp.bfloat16)
            out.append(
                send(p.at[to, pl.ds(2 * d, 2)], rr.at[2, d], rs_send.at[axis, 2, d], rs_recv.at[axis, 2, d], along(to))
            )
        return out

    def gathered(axis, k):
        p, rr = axes[axis][:2]
        left, right = (2, 1) if k < 2 else (1, 2)
        acc = p[0, k].astype(jnp.float32)
        acc = acc + rr[left, 0, k % 2].astype(jnp.float32)
        return acc + rr[right, 1, k % 2].astype(jnp.float32)

    blocks(4, lambda i: (i, 2))
    far_y = two_away(1)
    blocks(3, lambda i: (2, i + i // 2))
    far_x = two_away(0)
    blocks(6, lambda i: (1 + 2 * (i // 3), i % 3 + (i % 3) // 2))
    near_x = plain(0)
    blocks(3, lambda i: (0, i + i // 2))
    near_y = plain(1)

    g_copies = []
    for k in range(1, GROUPS):
        g_copies.append(
            send(h_src.at[(r + k) % GROUPS], g_dst.at[k], g_send.at[k], g_recv.at[k], along_r(k))
        )

    near_y += added(1, far_y)
    near_x += added(0, far_x)

    for copy in g_copies:
        copy.wait_recv()
    cut = h_src[r].astype(jnp.float32)
    for k in range(1, GROUPS):
        cut = cut + g_dst[k].astype(jnp.float32)
    h_dst[r] = cut.astype(jnp.bfloat16)
    h_copies = [
        send(h_dst.at[r], h_dst.at[r], h_send.at[k], h_recv.at[k], along_r(k)) for k in range(1, GROUPS)
    ]

    z_w.wait_recv()
    w1_other = w_first(1, 1 - zh)

    for copy in near_x + near_y:
        copy.wait_recv()
    rs2 = []
    for k in (2, 1, 3):
        for axis in (0, 1):
            _, _, out, landing, _, along = axes[axis]
            out[k - 1] = gathered(axis, k).astype(jnp.bfloat16)
            rs2.append(
                send(out.at[k - 1], landing.at[k - 1], rs2_send.at[axis, k - 1], rs2_recv.at[axis, k - 1], along(k))
            )

    for copy in w1_own:
        copy.wait_recv()
    w2_own = w_second(0, zh)
    for copy in w1_other:
        copy.wait_recv()
    w2_other = w_second(1, 1 - zh)
    wc = w_core(0, zh, 0) + w_core(1, 1 - zh, 0)

    loads[4].wait()
    loads[5].wait()
    for copy in h_copies:
        copy.wait_recv()
    for j in range(GROUPS):
        g_wide[j * CUT:(j + 1) * CUT, :] = h_dst[j].astype(jnp.float32)[0:CUT]
    average = g_wide[...] / GROUPS
    new_moment = outer_beta * mom_buf[...] + average
    moment_out[...] = new_moment
    params_out[...] = par_buf[...] - outer_rate * (average + outer_beta * new_moment)

    for copy in rs2:
        copy.wait_recv()
    for axis in (0, 1):
        acc = gathered(axis, 0)
        for j in range(3):
            acc = acc + axes[axis][3][j].astype(jnp.float32)
        total[:, axis * PART:(axis + 1) * PART] = acc.T
    other = pl.ds(pl.multiple_of((1 - zh) * 2 * ROWS, 16), 2 * ROWS)
    z_src[...] = total[other, :].astype(jnp.bfloat16)
    z_g = send(z_src, z_dst, z_send.at[1], z_recv.at[1], across)

    w3_own, more = w_third(0, zh, w2_own)
    wc += more
    w3_other, more = w_third(1, 1 - zh, w2_other)
    wc += more
    for s, plane, copies in ((0, zh, w3_own), (1, 1 - zh, w3_other)):
        for copy in copies:
            copy.wait_recv()
        wc += w_core(s, plane, 2)
    for copy in wc:
        copy.wait_recv()
    own_c = c_buf[0]

    def row(j, _):
        def col(i, _):
            blk = lax.dot_general(
                own_c, w_buf[j, i], (((1,), (1,)), ((), ())), preferred_element_type=jnp.float32
            )
            gi_out[:, pl.ds(pl.multiple_of((j * 4 + i) * BLOCK, 128), BLOCK)] = blk.astype(jnp.bfloat16)
            return 0

        return lax.fori_loop(0, 4, col, 0)

    lax.fori_loop(0, 4, row, 0)

    z_g.wait_recv()
    first = pl.multiple_of(zh * 2 * ROWS, 16)
    theirs = pl.multiple_of((1 - c) * ROWS, 16)
    ours = pl.multiple_of(c * ROWS, 16)
    swap[...] = total[pl.ds(first + theirs, ROWS), :] + z_dst[pl.ds(theirs, ROWS), :].astype(jnp.float32)
    sw = send(swap, gw_out.at[:, mine], core_send.at[1], core_recv.at[1], peer)
    gw_out[:, mine] = total[pl.ds(first + ours, ROWS), :] + z_dst[pl.ds(ours, ROWS), :].astype(jnp.float32)
    sw.wait_recv()

    for copy in sent:
        copy.wait_send()
    for j, k in A_ORDER:
        a_one(j, k).wait_send()


def store(*refs):
    sems = refs[8]
    copies = [pltpu.make_async_copy(refs[i], refs[4 + i], sems.at[i]) for i in range(4)]
    for copy in copies:
        copy.start()
    for copy in copies:
        copy.wait()


def body(activations, up_cotangent, up_weight, pseudo_grads, outer_params, outer_moment):
    bf16, f32 = jnp.bfloat16, jnp.float32
    dma = pltpu.SemaphoreType.DMA
    any_space = pl.BlockSpec(memory_space=pl.ANY)
    shapes = (((TOK, D), bf16), ((ROWS, FW), f32), ((ROWS, FRAG), f32), ((ROWS, FRAG), f32))
    vmem = pl.BlockSpec(memory_space=pltpu.VMEM)
    results = pl.pallas_call(
        kernel,
        out_shape=tuple(pltpu.VMEM(*shape) for shape in shapes),
        in_specs=[any_space] * 6,
        out_specs=(vmem,) * 4,
        scratch_shapes=[
            pltpu.VMEM((2 * TOK, D), bf16),
            pltpu.VMEM((2, TOK, FW), bf16),
            pltpu.VMEM((HALF, 2 * TOK), bf16),
            pltpu.VMEM((4, 4, PART, BLOCK), bf16),
            pltpu.VMEM((4, 4, PART, BLOCK), bf16),
            pltpu.VMEM((3, 2, 2, PART, BLOCK), bf16),
            pltpu.VMEM((3, 2, 2, PART, BLOCK), bf16),
            pltpu.VMEM((3, PART, BLOCK), bf16),
            pltpu.VMEM((3, PART, BLOCK), bf16),
            pltpu.VMEM((3, PART, BLOCK), bf16),
            pltpu.VMEM((3, PART, BLOCK), bf16),
            pltpu.VMEM((BLOCK, HALF), f32),
            pltpu.VMEM((2 * ROWS, HALF), bf16),
            pltpu.VMEM((2 * ROWS, HALF), bf16),
            pltpu.VMEM((ROWS, HALF), f32),
            pltpu.VMEM((4, 4, BLOCK, FW), bf16),
            pltpu.VMEM((ROWS, FRAG), bf16),
            pltpu.VMEM((ROWS, FRAG), f32),
            pltpu.VMEM((GROUPS, PAD, FRAG), f32),
            pltpu.VMEM((GROUPS, PAD, FRAG), bf16),
            pltpu.VMEM((GROUPS, PAD, FRAG), bf16),
            pltpu.VMEM((GROUPS, PAD, FRAG), bf16),
            pltpu.VMEM((ROWS, FRAG), f32),
            pltpu.VMEM((ROWS, FRAG), f32),
            dma((6,)),
            dma((2,)),
            dma((2,)),
            dma((4, 4)),
            dma((4, 4)),
            dma((2, 3, 2)),
            dma((2, 3, 2)),
            dma((2, 3)),
            dma((2, 3)),
            dma((2,)),
            dma((2,)),
            dma((2, 2, 3)),
            dma((2, 2, 3)),
            dma((2, 2, 2, 2)),
            dma((2, 2, 2, 2)),
            dma((2, 2, 4)),
            dma((2, 2, 4)),
            dma((GROUPS,)),
            dma((GROUPS,)),
            dma((GROUPS,)),
            dma((GROUPS,)),
        ],
        compiler_params=pltpu.CompilerParams(
            collective_id=0, has_side_effects=True, vmem_limit_bytes=61 * 1024 * 1024
        ),
        cost_estimate=pl.CostEstimate(flops=2 * 2 * TOK * D * FW, bytes_accessed=8 << 20, transcendentals=0),
        name="up_backward",
    )(
        activations[0], up_cotangent[0], up_weight[0], pseudo_grads[0], outer_params, outer_moment
    )
    gi, gw, new_params, new_moment = pl.pallas_call(
        store,
        out_shape=tuple(jax.ShapeDtypeStruct(*shape) for shape in shapes),
        in_specs=[vmem] * 4,
        out_specs=(any_space,) * 4,
        scratch_shapes=[dma((4,))],
        name="store_results",
    )(*results)
    return gi[None], gw[None], new_params, new_moment


def solution(mesh):
    placed = (
        P("replica", "fsdp", None),
        P("replica", "fsdp", None),
        P("replica", "fsdp", None),
        P("replica", "fsdp", None),
        P("fsdp", None),
        P("fsdp", None),
    )
    return jax.shard_map(
        body,
        mesh=mesh,
        in_specs=placed,
        out_specs=(
            P("replica", "fsdp", None),
            P("replica", "fsdp", None),
            P("fsdp", None),
            P("fsdp", None),
        ),
        check_vma=False,
    )
```

```python
import jax
import jax.numpy as jnp
from jax import lax
from jax.experimental import pallas as pl
from jax.experimental.pallas import tpu as pltpu
from jax.sharding import PartitionSpec as P

outer_rate = 0.7
outer_beta = 0.9

SIDE = 4
GROUPS = 8
TOK = 128
ROWS = 96
D = 6144
FW = 512
HALF = FW // 2
PART = HALF // 2
BLOCK = 4 * ROWS
FRAG = 384
CUT = ROWS // GROUPS
PAD = 16
HROWS = ROWS // 2

MESH = pl.DeviceIdType.MESH
ORDER = (1, 3, 2)
TWO_AWAY = ((2, 2), (0, 2), (2, 0), (1, 2), (2, 1), (3, 2), (2, 3))
PLAIN = ((1, 3), (3, 1), (3, 0), (0, 3))
REST = ((1, 0), (1, 1), (3, 3), (0, 1), (0, 0))
A_ORDER = TWO_AWAY + PLAIN + REST
PIECE = PART // 2


def kernel(
    act, cot, weight, pseudo, params, moment,
    gi_out, gw_out, params_out, moment_out,
    a_buf, c_buf, ct_buf, p_x, p_y, r_x, r_y, s_x, s_y, q_x, q_y, total, z_src, z_dst, swapped, gw_buf,
    w_buf, gi_buf, g_buf, g_wide, g_src, g_dst, h_src, h_dst, par_buf, mom_buf,
    load_sem, store_sem, core_send, core_recv, a_send, a_recv, rs_send, rs_recv, rs2_send, rs2_recv, z_send, z_recv,
    w1_send, w1_recv, w2_send, w2_recv, wc_send, wc_recv, g_send, g_recv, h_send, h_recv,
):
    r = lax.axis_index("replica")
    f = lax.axis_index("fsdp")
    y, x, zh, c = f // 16, (f // 4) % 4, (f // 2) % 2, f % 2

    def at(y, x, zh, c):
        return (r, ((y * 4 + x) * 2 + zh) * 2 + c)

    def along_x(k):
        return at(y, (x + k) % 4, zh, c)

    def along_y(k):
        return at((y + k) % 4, x, zh, c)

    def along_r(k):
        return ((r + k) % GROUPS, f)

    peer = at(y, x, zh, 1 - c)
    across = at(y, x, 1 - zh, c)

    sent = []

    def send(src, dst, ss, rs, to):
        copy = pltpu.make_async_remote_copy(
            src_ref=src, dst_ref=dst, send_sem=ss, recv_sem=rs, device_id=to, device_id_type=MESH
        )
        copy.start()
        sent.append(copy)
        return copy

    own_w = w_buf.at[y, x, pl.ds(pl.multiple_of((zh * 2 + c) * ROWS, ROWS), ROWS)]
    loads = [
        pltpu.make_async_copy(weight, own_w, load_sem.at[0]),
        pltpu.make_async_copy(cot, c_buf.at[0], load_sem.at[1]),
        pltpu.make_async_copy(act, a_buf.at[pl.ds(0, TOK)], load_sem.at[2]),
        pltpu.make_async_copy(pseudo, g_buf, load_sem.at[3]),
        pltpu.make_async_copy(params, par_buf, load_sem.at[4]),
        pltpu.make_async_copy(moment, mom_buf, load_sem.at[5]),
    ]
    for copy in loads:
        copy.start()

    barrier = pltpu.get_barrier_semaphore()
    friends = [peer, across, at(y, x, 1 - zh, 1 - c)]
    friends += [along_x(k) for k in ORDER] + [along_y(k) for k in ORDER]
    friends += [along_r(k) for k in range(1, GROUPS)]
    for to in friends:
        pl.semaphore_signal(barrier, inc=1, device_id=to, device_id_type=MESH)

    loads[3].wait()
    g_wide[...] = g_buf[...].astype(jnp.float32)
    for j in range(GROUPS):
        g_src[j, 0:CUT, :] = g_wide[j * CUT:(j + 1) * CUT, :]
        g_src[j, CUT:PAD, :] = jnp.zeros((PAD - CUT, FRAG), jnp.float32)
    for j in range(GROUPS):
        h_src[j] = g_src[j].astype(jnp.bfloat16)
    loads[0].wait()
    loads[1].wait()
    loads[2].wait()
    pl.semaphore_wait(barrier, len(friends))

    z_w = []
    for i in range(2):
        ref = w_buf.at[y, x, pl.ds(pl.multiple_of((zh * 2 + c) * ROWS + i * HROWS, 16), HROWS)]
        z_w.append(send(ref, ref, z_send.at[2 + i], z_recv.at[2 + i], across))
    c_copy = send(c_buf.at[0], c_buf.at[1], core_send.at[0], core_recv.at[0], peer)

    def a_cols(j, k):
        return pl.ds(pl.multiple_of((((y + k) % 4) * 4 + (x + j) % 4) * BLOCK, 128), BLOCK)

    def a_one(j, k):
        return pltpu.make_async_remote_copy(
            src_ref=a_buf.at[pl.ds(0, TOK), a_cols(j, k)], dst_ref=a_buf.at[pl.ds(TOK, TOK), a_cols(j, k)],
            send_sem=a_send.at[j, k], recv_sem=a_recv.at[j, k], device_id=peer, device_id_type=MESH,
        )

    for j, k in A_ORDER:
        a_one(j, k).start()

    def w_rows(plane, second):
        return pl.ds(pl.multiple_of((plane * 2 + c) * ROWS + second * HROWS, 16), HROWS)

    def w_first(s, plane):
        copies = []
        for k in ORDER:
            ref = w_buf.at[y, x, w_rows(plane, 0)]
            copies.append(send(ref, ref, w1_send.at[s, 0, k - 1], w1_recv.at[s, 0, k - 1], along_x(k)))
            ref = w_buf.at[y, x, w_rows(plane, 1)]
            copies.append(send(ref, ref, w1_send.at[s, 1, k - 1], w1_recv.at[s, 1, k - 1], along_y(k)))
        return copies

    def w_second(s, plane, pieces):
        copies = {}
        for i in pieces:
            for d, to in ((0, 1), (1, 3)):
                ref = w_buf.at[y, (x + i) % 4, w_rows(plane, 0)]
                copies[0, d, i] = send(
                    ref, ref, w2_send.at[s, 0, 0, d, i], w2_recv.at[s, 0, 0, d, i], along_y(to)
                )
                ref = w_buf.at[(y + i) % 4, x, w_rows(plane, 1)]
                copies[1, d, i] = send(
                    ref, ref, w2_send.at[s, 1, 0, d, i], w2_recv.at[s, 1, 0, d, i], along_x(to)
                )
        return copies

    def w_third(s, plane, copies):
        out, core = [], []
        for i in range(4):
            d, to = ((0, 1), (1, 3))[i // 2]
            copies[0, d, i].wait_recv()
            ref = w_buf.at[(y - to) % 4, (x + i) % 4, w_rows(plane, 0)]
            out.append(send(ref, ref, w2_send.at[s, 0, 1, d, i], w2_recv.at[s, 0, 1, d, i], along_y(to)))
            copies[1, d, i].wait_recv()
            ref = w_buf.at[(y + i) % 4, (x - to) % 4, w_rows(plane, 1)]
            out.append(send(ref, ref, w2_send.at[s, 1, 1, d, i], w2_recv.at[s, 1, 1, d, i], along_x(to)))
        for i in range(4):
            copies[0, 1 - i // 2, i].wait_recv()
            copies[1, 1 - i // 2, i].wait_recv()
        for k in (1, 3):
            core += w_core(s, plane, k)
        return out, core

    def w_core(s, plane, k):
        ref = w_buf.at[(y - k) % 4, :, w_rows(plane, 0)]
        one = send(ref, ref, wc_send.at[s, 0, k], wc_recv.at[s, 0, k], peer)
        ref = w_buf.at[:, (x - k) % 4, w_rows(plane, 1)]
        two = send(ref, ref, wc_send.at[s, 1, k], wc_recv.at[s, 1, k], peer)
        return [one, two]

    w1_own = w_first(0, zh)
    w2_own = w_second(0, zh, (0,))

    c_copy.wait_recv()
    mine = pl.ds(pl.multiple_of(c * HALF, HALF), HALF)
    ct_buf[:, 0:TOK] = c_buf[0, :, mine].T
    ct_buf[:, TOK:2 * TOK] = c_buf[1, :, mine].T

    axes = ((p_x, r_x, s_x, q_x, along_x, along_y), (p_y, r_y, s_y, q_y, along_y, along_x))
    half = (pl.ds(0, PIECE), pl.ds(PIECE, PIECE))
    rs = {}

    def leave(axis, step, d, j, h):
        p, rr, _, _, along, _ = axes[axis]
        to = (1, 3)[d]
        near = 2 if step == 0 else to
        k = 2 * d + j if step != 1 else 2 - 2 * d + j
        rs[axis, step, d, j, h] = send(
            p.at[near, k, half[h]], rr.at[step, d, j, half[h]],
            rs_send.at[axis, step, d, 2 * j + h], rs_recv.at[axis, step, d, 2 * j + h], along(to),
        )

    def block(j, k):
        a_one(j, k).wait_recv()
        part = jnp.dot(ct_buf[...], a_buf[:, a_cols(j, k)], preferred_element_type=jnp.float32)
        part = part.astype(jnp.bfloat16)
        p_x[j, k] = part[0:PART]
        p_y[k, j] = part[PART:HALF]

    def leave_block(axis, near, far):
        for h in range(2):
            if near == 2:
                leave(axis, 0, far // 2, far % 2, h)
            elif near == 1 and far >= 2:
                leave(axis, 1, 0, far % 2, h)
            elif near == 3 and far < 2:
                leave(axis, 1, 1, far % 2, h)

    def gathered(axis, k):
        p, rr = axes[axis][:2]
        left, right = (2, 1) if k < 2 else (1, 2)
        acc = p[0, k].astype(jnp.float32)
        acc = acc + rr[left, 0, k % 2].astype(jnp.float32)
        return acc + rr[right, 1, k % 2].astype(jnp.float32)

    def arrived(axis, k):
        left, right = (2, 1) if k < 2 else (1, 2)
        for h in range(2):
            rs[axis, left, 0, k % 2, h].wait_recv()
            rs[axis, right, 1, k % 2, h].wait_recv()

    for j, k in TWO_AWAY:
        block(j, k)
        if k == 2:
            leave_block(1, 2, j)
        if j == 2:
            leave_block(0, 2, k)
    for j, k in ((1, 2), (3, 2), (2, 1), (2, 3)) + PLAIN:
        if (j, k) in PLAIN:
            block(j, k)
        if j != 2:
            leave_block(0, j, k)
        if k != 2:
            leave_block(1, k, j)
    for j, k in REST:
        block(j, k)

    g_copies = []
    for k in range(1, GROUPS):
        g_copies.append(
            send(h_src.at[(r + k) % GROUPS], g_dst.at[k], g_send.at[k], g_recv.at[k], along_r(k))
        )

    for d, j in ((1, 0), (0, 0), (0, 1), (1, 1)):
        for h in range(2):
            for axis in (1, 0):
                p, rr = axes[axis][:2]
                rs[axis, 0, d, j, h].wait_recv()
                to = (1, 3)[d]
                acc = p[to, 2 * d + j, half[h], :].astype(jnp.float32) + rr[0, d, j, half[h], :].astype(jnp.float32)
                p[to, 2 * d + j, half[h], :] = acc.astype(jnp.bfloat16)
                leave(axis, 2, d, j, h)

    for copy in w1_own:
        copy.wait_recv()
    w2_own.update(w_second(0, zh, (1, 2, 3)))
    wc = w_core(0, zh, 0)

    rs2 = []
    for k in (2, 1, 3):
        for axis in (1, 0):
            _, _, out, landing, _, along = axes[axis]
            arrived(axis, k)
            out[k - 1] = gathered(axis, k).astype(jnp.bfloat16)
            for h in range(2):
                rs2.append(
                    send(
                        out.at[k - 1, half[h]], landing.at[k - 1, half[h]],
                        rs2_send.at[axis, k - 1, h], rs2_recv.at[axis, k - 1, h], along(k),
                    )
                )

    for copy in g_copies:
        copy.wait_recv()
    cut = h_src[r].astype(jnp.float32)
    for k in range(1, GROUPS):
        cut = cut + g_dst[k].astype(jnp.float32)
    h_dst[r] = cut.astype(jnp.bfloat16)
    h_copies = [
        send(h_dst.at[r], h_dst.at[r], h_send.at[k], h_recv.at[k], along_r(k)) for k in range(1, GROUPS)
    ]

    for copy in z_w:
        copy.wait_recv()
    w1_other = w_first(1, 1 - zh)
    w2_other = w_second(1, 1 - zh, (0,))
    w3_own, more = w_third(0, zh, w2_own)
    wc += more

    for copy in rs2:
        copy.wait_recv()
    for axis in (0, 1):
        arrived(axis, 0)
        acc = gathered(axis, 0)
        for j in range(3):
            acc = acc + axes[axis][3][j].astype(jnp.float32)
        total[:, axis * PART:(axis + 1) * PART] = acc.T

    def rows(plane, core):
        return pl.ds(pl.multiple_of((plane * 2 + core) * ROWS, 16), ROWS)

    z_g = []
    for i, core in enumerate((c, 1 - c)):
        z_src[i] = total[rows(1 - zh, core), :].astype(jnp.bfloat16)
        z_g.append(
            send(z_src.at[i], z_dst.at[i], z_send.at[i], z_recv.at[i], at(y, x, 1 - zh, core))
        )
    swap = send(total.at[rows(zh, 1 - c)], swapped, core_send.at[1], core_recv.at[1], peer)

    for copy in w1_other:
        copy.wait_recv()
    w2_other.update(w_second(1, 1 - zh, (1, 2, 3)))
    wc += w_core(1, 1 - zh, 0)
    for copy in w3_own:
        copy.wait_recv()
    w_last = w_core(0, zh, 2)

    loads[4].wait()
    loads[5].wait()
    for copy in h_copies:
        copy.wait_recv()
    for j in range(GROUPS):
        g_wide[j * CUT:(j + 1) * CUT, :] = h_dst[j].astype(jnp.float32)[0:CUT]
    average = g_wide[...] / GROUPS
    new_moment = outer_beta * mom_buf[...] + average
    mom_buf[...] = new_moment
    par_buf[...] = par_buf[...] - outer_rate * (average + outer_beta * new_moment)
    stores = [
        pltpu.make_async_copy(par_buf, params_out, store_sem.at[0]),
        pltpu.make_async_copy(mom_buf, moment_out, store_sem.at[1]),
    ]
    for copy in stores:
        copy.start()

    w3_other, more = w_third(1, 1 - zh, w2_other)
    wc += more
    own_c = c_buf[0]

    def gi_block(j, k):
        blk = lax.dot_general(
            own_c, w_buf[(y + k) % 4, (x + j) % 4], (((1,), (1,)), ((), ())), preferred_element_type=jnp.float32
        )
        gi_buf[:, a_cols(j, k)] = blk.astype(jnp.bfloat16)

    for copy in wc:
        copy.wait_recv()
    for k in (0, 1, 3):
        for j in (0, 1, 3):
            gi_block(j, k)
    for copy in w3_other:
        copy.wait_recv()
    w_last += w_core(1, 1 - zh, 2)
    for copy in w_last:
        copy.wait_recv()
    for j in range(4):
        gi_block(j, 2)
    for k in (0, 1, 3):
        gi_block(2, k)
    stores.append(pltpu.make_async_copy(gi_buf, gi_out, store_sem.at[2]))
    stores[2].start()

    swap.wait_recv()
    for copy in z_g:
        copy.wait_recv()
    gw_buf[:, mine] = total[rows(zh, c), :] + z_dst[0].astype(jnp.float32)
    others = pl.ds(pl.multiple_of((1 - c) * HALF, HALF), HALF)
    gw_buf[:, others] = swapped[...] + z_dst[1].astype(jnp.float32)
    stores.append(pltpu.make_async_copy(gw_buf, gw_out, store_sem.at[3]))
    stores[3].start()

    for copy in sent:
        copy.wait_send()
    for j, k in A_ORDER:
        a_one(j, k).wait_send()
    for copy in stores:
        copy.wait()


def store(gi, gw, params, moment, gi_out, gw_out, params_out, moment_out, gi_buf, gw_buf, par_buf, mom_buf, sem):
    pieces = [
        (ref.at[pl.ds(i * 32, 32)], buf.at[pl.ds(i * 32, 32)], out.at[pl.ds(i * 32, 32)])
        for ref, buf, out in ((gi, gi_buf, gi_out),)
        for i in range(TOK // 32)
    ]
    pieces += [(gw, gw_buf, gw_out), (params, par_buf, params_out), (moment, mom_buf, moment_out)]
    loads = [pltpu.make_async_copy(p[0], p[1], sem.at[0, i]) for i, p in enumerate(pieces)]
    stores = [pltpu.make_async_copy(p[1], p[2], sem.at[1, i]) for i, p in enumerate(pieces)]
    for copy in loads:
        copy.start()
    for i in range(len(pieces)):
        loads[i].wait()
        stores[i].start()
    for copy in stores:
        copy.wait()


def body(activations, up_cotangent, up_weight, pseudo_grads, outer_params, outer_moment):
    bf16, f32 = jnp.bfloat16, jnp.float32
    dma = pltpu.SemaphoreType.DMA
    any_space = pl.BlockSpec(memory_space=pl.ANY)
    shapes = (((TOK, D), bf16), ((ROWS, FW), f32), ((ROWS, FRAG), f32), ((ROWS, FRAG), f32))
    results = pl.pallas_call(
        kernel,
        out_shape=tuple(jax.ShapeDtypeStruct(*shape) for shape in shapes),
        in_specs=[any_space] * 6,
        out_specs=(any_space,) * 4,
        scratch_shapes=[
            pltpu.VMEM((2 * TOK, D), bf16),
            pltpu.VMEM((2, TOK, FW), bf16),
            pltpu.VMEM((HALF, 2 * TOK), bf16),
            pltpu.VMEM((4, 4, PART, BLOCK), bf16),
            pltpu.VMEM((4, 4, PART, BLOCK), bf16),
            pltpu.VMEM((3, 2, 2, PART, BLOCK), bf16),
            pltpu.VMEM((3, 2, 2, PART, BLOCK), bf16),
            pltpu.VMEM((3, PART, BLOCK), bf16),
            pltpu.VMEM((3, PART, BLOCK), bf16),
            pltpu.VMEM((3, PART, BLOCK), bf16),
            pltpu.VMEM((3, PART, BLOCK), bf16),
            pltpu.VMEM((BLOCK, HALF), f32),
            pltpu.VMEM((2, ROWS, HALF), bf16),
            pltpu.VMEM((2, ROWS, HALF), bf16),
            pltpu.VMEM((ROWS, HALF), f32),
            pltpu.VMEM((ROWS, FW), f32),
            pltpu.VMEM((4, 4, BLOCK, FW), bf16),
            pltpu.VMEM((TOK, D), bf16),
            pltpu.VMEM((ROWS, FRAG), bf16),
            pltpu.VMEM((ROWS, FRAG), f32),
            pltpu.VMEM((GROUPS, PAD, FRAG), f32),
            pltpu.VMEM((GROUPS, PAD, FRAG), bf16),
            pltpu.VMEM((GROUPS, PAD, FRAG), bf16),
            pltpu.VMEM((GROUPS, PAD, FRAG), bf16),
            pltpu.VMEM((ROWS, FRAG), f32),
            pltpu.VMEM((ROWS, FRAG), f32),
            dma((6,)),
            dma((4,)),
            dma((2,)),
            dma((2,)),
            dma((4, 4)),
            dma((4, 4)),
            dma((2, 3, 2, 4)),
            dma((2, 3, 2, 4)),
            dma((2, 3, 2)),
            dma((2, 3, 2)),
            dma((4,)),
            dma((4,)),
            dma((2, 2, 3)),
            dma((2, 2, 3)),
            dma((2, 2, 2, 2, 4)),
            dma((2, 2, 2, 2, 4)),
            dma((2, 2, 4)),
            dma((2, 2, 4)),
            dma((GROUPS,)),
            dma((GROUPS,)),
            dma((GROUPS,)),
            dma((GROUPS,)),
        ],
        compiler_params=pltpu.CompilerParams(
            collective_id=0, has_side_effects=True, vmem_limit_bytes=62 * 1024 * 1024
        ),
        cost_estimate=pl.CostEstimate(flops=2 * 2 * TOK * D * FW, bytes_accessed=8 << 20, transcendentals=0),
        name="up_backward",
    )(
        activations[0], up_cotangent[0], up_weight[0], pseudo_grads[0], outer_params, outer_moment
    )
    gi, gw, new_params, new_moment = pl.pallas_call(
        store,
        out_shape=tuple(jax.ShapeDtypeStruct(*shape) for shape in shapes),
        in_specs=[any_space] * 4,
        out_specs=(any_space,) * 4,
        scratch_shapes=[pltpu.VMEM(*shape) for shape in shapes] + [dma((2, TOK // 32 + 3))],
        compiler_params=pltpu.CompilerParams(vmem_limit_bytes=62 * 1024 * 1024),
        name="store_results",
    )(*results)
    return gi[None], gw[None], new_params, new_moment


def solution(mesh):
    placed = (
        P("replica", "fsdp", None),
        P("replica", "fsdp", None),
        P("replica", "fsdp", None),
        P("replica", "fsdp", None),
        P("fsdp", None),
        P("fsdp", None),
    )
    return jax.shard_map(
        body,
        mesh=mesh,
        in_specs=placed,
        out_specs=(
            P("replica", "fsdp", None),
            P("replica", "fsdp", None),
            P("fsdp", None),
            P("fsdp", None),
        ),
        check_vma=False,
    )
```

```python
import jax
import jax.numpy as jnp
from jax import lax
from jax.experimental import pallas as pl
from jax.experimental.pallas import tpu as pltpu
from jax.sharding import PartitionSpec as P

outer_rate = 0.7
outer_beta = 0.9

SIDE = 4
GROUPS = 8
TOK = 128
ROWS = 96
D = 6144
FW = 512
HALF = FW // 2
PART = HALF // 2
BLOCK = 4 * ROWS
FRAG = 384
CUT = ROWS // GROUPS
PAD = 16
HROWS = ROWS // 2

MESH = pl.DeviceIdType.MESH
ORDER = (1, 3, 2)
TWO_AWAY = ((2, 2), (0, 2), (2, 0), (1, 2), (2, 1), (3, 2), (2, 3))
PLAIN = ((1, 3), (3, 1), (3, 0), (0, 3))
REST = ((1, 0), (1, 1), (3, 3), (0, 1), (0, 0))
A_ORDER = TWO_AWAY + PLAIN + REST
PIECE = PART // 2


def kernel(
    act, cot, weight, pseudo, params, moment,
    gi_out, gw_out, params_out, moment_out,
    a_buf, c_buf, ct_buf, p_x, p_y, r_x, r_y, s_x, s_y, q_x, q_y, total, z_src, z_dst, swapped, gw_buf,
    w_buf, gi_buf, g_buf, g_wide, g_src, g_dst, h_src, h_dst, par_buf, mom_buf,
    load_sem, store_sem, core_send, core_recv, a_send, a_recv, rs_send, rs_recv, rs2_send, rs2_recv, z_send, z_recv,
    w1_send, w1_recv, w2_send, w2_recv, wc_send, wc_recv, g_send, g_recv, h_send, h_recv,
):
    r = lax.axis_index("replica")
    f = lax.axis_index("fsdp")
    y, x, zh, c = f // 16, (f // 4) % 4, (f // 2) % 2, f % 2

    def at(y, x, zh, c):
        return (r, ((y * 4 + x) * 2 + zh) * 2 + c)

    def along_x(k):
        return at(y, (x + k) % 4, zh, c)

    def along_y(k):
        return at((y + k) % 4, x, zh, c)

    def along_r(k):
        return ((r + k) % GROUPS, f)

    peer = at(y, x, zh, 1 - c)
    across = at(y, x, 1 - zh, c)

    sent = []

    def send(src, dst, ss, rs, to):
        copy = pltpu.make_async_remote_copy(
            src_ref=src, dst_ref=dst, send_sem=ss, recv_sem=rs, device_id=to, device_id_type=MESH
        )
        copy.start()
        sent.append(copy)
        return copy

    own_w = w_buf.at[y, x, pl.ds(pl.multiple_of((zh * 2 + c) * ROWS, ROWS), ROWS)]
    loads = [
        pltpu.make_async_copy(weight, own_w, load_sem.at[0]),
        pltpu.make_async_copy(cot, c_buf.at[0], load_sem.at[1]),
        pltpu.make_async_copy(act, a_buf.at[pl.ds(0, TOK)], load_sem.at[2]),
        pltpu.make_async_copy(pseudo, g_buf, load_sem.at[3]),
        pltpu.make_async_copy(params, par_buf, load_sem.at[4]),
        pltpu.make_async_copy(moment, mom_buf, load_sem.at[5]),
    ]
    for copy in loads:
        copy.start()

    barrier = pltpu.get_barrier_semaphore()
    friends = [peer, across, at(y, x, 1 - zh, 1 - c)]
    friends += [along_x(k) for k in ORDER] + [along_y(k) for k in ORDER]
    friends += [along_r(k) for k in range(1, GROUPS)]
    for to in friends:
        pl.semaphore_signal(barrier, inc=1, device_id=to, device_id_type=MESH)

    loads[3].wait()
    g_wide[...] = g_buf[...].astype(jnp.float32)
    for j in range(GROUPS):
        g_src[j, 0:CUT, :] = g_wide[j * CUT:(j + 1) * CUT, :]
        g_src[j, CUT:PAD, :] = jnp.zeros((PAD - CUT, FRAG), jnp.float32)
    for j in range(GROUPS):
        h_src[j] = g_src[j].astype(jnp.bfloat16)
    loads[0].wait()
    loads[1].wait()
    loads[2].wait()
    pl.semaphore_wait(barrier, len(friends))

    z_w = []
    for i in range(2):
        ref = w_buf.at[y, x, pl.ds(pl.multiple_of((zh * 2 + c) * ROWS + i * HROWS, 16), HROWS)]
        z_w.append(send(ref, ref, z_send.at[2 + i], z_recv.at[2 + i], across))
    c_copy = send(c_buf.at[0], c_buf.at[1], core_send.at[0], core_recv.at[0], peer)

    def a_cols(j, k):
        return pl.ds(pl.multiple_of((((y + k) % 4) * 4 + (x + j) % 4) * BLOCK, 128), BLOCK)

    def a_one(j, k):
        return pltpu.make_async_remote_copy(
            src_ref=a_buf.at[pl.ds(0, TOK), a_cols(j, k)], dst_ref=a_buf.at[pl.ds(TOK, TOK), a_cols(j, k)],
            send_sem=a_send.at[j, k], recv_sem=a_recv.at[j, k], device_id=peer, device_id_type=MESH,
        )

    for j, k in A_ORDER:
        a_one(j, k).start()

    def w_rows(plane, second):
        return pl.ds(pl.multiple_of((plane * 2 + c) * ROWS + second * HROWS, 16), HROWS)

    def w_first(s, plane):
        copies = []
        for k in ORDER:
            ref = w_buf.at[y, x, w_rows(plane, 0)]
            copies.append(send(ref, ref, w1_send.at[s, 0, k - 1], w1_recv.at[s, 0, k - 1], along_x(k)))
            ref = w_buf.at[y, x, w_rows(plane, 1)]
            copies.append(send(ref, ref, w1_send.at[s, 1, k - 1], w1_recv.at[s, 1, k - 1], along_y(k)))
        return copies

    def w_second(s, plane, pieces):
        copies = {}
        for i in pieces:
            for d, to in ((0, 1), (1, 3)):
                ref = w_buf.at[y, (x + i) % 4, w_rows(plane, 0)]
                copies[0, d, i] = send(
                    ref, ref, w2_send.at[s, 0, 0, d, i], w2_recv.at[s, 0, 0, d, i], along_y(to)
                )
                ref = w_buf.at[(y + i) % 4, x, w_rows(plane, 1)]
                copies[1, d, i] = send(
                    ref, ref, w2_send.at[s, 1, 0, d, i], w2_recv.at[s, 1, 0, d, i], along_x(to)
                )
        return copies

    def w_third(s, plane, copies):
        out, core = [], []
        for i in range(4):
            d, to = ((0, 1), (1, 3))[i // 2]
            copies[0, d, i].wait_recv()
            ref = w_buf.at[(y - to) % 4, (x + i) % 4, w_rows(plane, 0)]
            out.append(send(ref, ref, w2_send.at[s, 0, 1, d, i], w2_recv.at[s, 0, 1, d, i], along_y(to)))
            copies[1, d, i].wait_recv()
            ref = w_buf.at[(y + i) % 4, (x - to) % 4, w_rows(plane, 1)]
            out.append(send(ref, ref, w2_send.at[s, 1, 1, d, i], w2_recv.at[s, 1, 1, d, i], along_x(to)))
        for i in range(4):
            copies[0, 1 - i // 2, i].wait_recv()
            copies[1, 1 - i // 2, i].wait_recv()
        for k in (1, 3):
            core += w_core(s, plane, k)
        return out, core

    def w_core(s, plane, k):
        ref = w_buf.at[(y - k) % 4, :, w_rows(plane, 0)]
        one = send(ref, ref, wc_send.at[s, 0, k], wc_recv.at[s, 0, k], peer)
        ref = w_buf.at[:, (x - k) % 4, w_rows(plane, 1)]
        two = send(ref, ref, wc_send.at[s, 1, k], wc_recv.at[s, 1, k], peer)
        return [one, two]

    w1_own = w_first(0, zh)
    w2_own = w_second(0, zh, (0,))

    c_copy.wait_recv()
    mine = pl.ds(pl.multiple_of(c * HALF, HALF), HALF)
    ct_buf[:, 0:TOK] = c_buf[0, :, mine].T
    ct_buf[:, TOK:2 * TOK] = c_buf[1, :, mine].T

    axes = ((p_x, r_x, s_x, q_x, along_x, along_y), (p_y, r_y, s_y, q_y, along_y, along_x))
    half = (pl.ds(0, PIECE), pl.ds(PIECE, PIECE))
    rs = {}

    def leave(axis, step, d, j, h):
        p, rr, _, _, along, _ = axes[axis]
        to = (1, 3)[d]
        near = 2 if step == 0 else to
        k = 2 * d + j if step != 1 else 2 - 2 * d + j
        rs[axis, step, d, j, h] = send(
            p.at[near, k, half[h]], rr.at[step, d, j, half[h]],
            rs_send.at[axis, step, d, 2 * j + h], rs_recv.at[axis, step, d, 2 * j + h], along(to),
        )

    def block(j, k):
        a_one(j, k).wait_recv()
        part = jnp.dot(ct_buf[...], a_buf[:, a_cols(j, k)], preferred_element_type=jnp.float32)
        part = part.astype(jnp.bfloat16)
        p_x[j, k] = part[0:PART]
        p_y[k, j] = part[PART:HALF]

    def leave_block(axis, near, far):
        for h in range(2):
            if near == 2:
                leave(axis, 0, far // 2, far % 2, h)
            elif near == 1 and far >= 2:
                leave(axis, 1, 0, far % 2, h)
            elif near == 3 and far < 2:
                leave(axis, 1, 1, far % 2, h)

    def gathered(axis, k):
        p, rr = axes[axis][:2]
        left, right = (2, 1) if k < 2 else (1, 2)
        acc = p[0, k].astype(jnp.float32)
        acc = acc + rr[left, 0, k % 2].astype(jnp.float32)
        return acc + rr[right, 1, k % 2].astype(jnp.float32)

    def arrived(axis, k):
        left, right = (2, 1) if k < 2 else (1, 2)
        for h in range(2):
            rs[axis, left, 0, k % 2, h].wait_recv()
            rs[axis, right, 1, k % 2, h].wait_recv()

    for j, k in TWO_AWAY:
        block(j, k)
        if k == 2:
            leave_block(1, 2, j)
        if j == 2:
            leave_block(0, 2, k)
    for j, k in ((1, 2), (3, 2), (2, 1), (2, 3)) + PLAIN:
        if (j, k) in PLAIN:
            block(j, k)
        if j != 2:
            leave_block(0, j, k)
        if k != 2:
            leave_block(1, k, j)
    for j, k in REST:
        block(j, k)

    g_copies = []
    for k in range(1, GROUPS):
        g_copies.append(
            send(h_src.at[(r + k) % GROUPS], g_dst.at[k], g_send.at[k], g_recv.at[k], along_r(k))
        )

    for d, j in ((1, 0), (0, 0), (0, 1), (1, 1)):
        for h in range(2):
            for axis in (1, 0):
                p, rr = axes[axis][:2]
                rs[axis, 0, d, j, h].wait_recv()
                to = (1, 3)[d]
                acc = p[to, 2 * d + j, half[h], :].astype(jnp.float32) + rr[0, d, j, half[h], :].astype(jnp.float32)
                p[to, 2 * d + j, half[h], :] = acc.astype(jnp.bfloat16)
                leave(axis, 2, d, j, h)

    for copy in z_w:
        copy.wait_recv()
    w1_other = w_first(1, 1 - zh)
    w2_other = w_second(1, 1 - zh, (0,))

    rs2 = []
    for k in (2, 1, 3):
        for axis in (1, 0):
            _, _, out, landing, _, along = axes[axis]
            arrived(axis, k)
            out[k - 1] = gathered(axis, k).astype(jnp.bfloat16)
            for h in range(2):
                rs2.append(
                    send(
                        out.at[k - 1, half[h]], landing.at[k - 1, half[h]],
                        rs2_send.at[axis, k - 1, h], rs2_recv.at[axis, k - 1, h], along(k),
                    )
                )

    for copy in w1_own:
        copy.wait_recv()
    w2_own.update(w_second(0, zh, (1, 2, 3)))
    wc = w_core(0, zh, 0)
    for copy in w1_other:
        copy.wait_recv()
    w2_other.update(w_second(1, 1 - zh, (1, 2, 3)))
    wc += w_core(1, 1 - zh, 0)

    for copy in g_copies:
        copy.wait_recv()
    cut = h_src[r].astype(jnp.float32)
    for k in range(1, GROUPS):
        cut = cut + g_dst[k].astype(jnp.float32)
    h_dst[r] = cut.astype(jnp.bfloat16)
    h_copies = [
        send(h_dst.at[r], h_dst.at[r], h_send.at[k], h_recv.at[k], along_r(k)) for k in range(1, GROUPS)
    ]

    for copy in rs2:
        copy.wait_recv()
    for axis in (0, 1):
        arrived(axis, 0)
        acc = gathered(axis, 0)
        for j in range(3):
            acc = acc + axes[axis][3][j].astype(jnp.float32)
        total[:, axis * PART:(axis + 1) * PART] = acc.T

    def rows(plane, core):
        return pl.ds(pl.multiple_of((plane * 2 + core) * ROWS, 16), ROWS)

    z_g = []
    for i, core in enumerate((c, 1 - c)):
        z_src[i] = total[rows(1 - zh, core), :].astype(jnp.bfloat16)
        z_g.append(
            send(z_src.at[i], z_dst.at[i], z_send.at[i], z_recv.at[i], at(y, x, 1 - zh, core))
        )
    swap = send(total.at[rows(zh, 1 - c)], swapped, core_send.at[1], core_recv.at[1], peer)

    w3_own, more = w_third(0, zh, w2_own)
    wc += more
    w3_other, more = w_third(1, 1 - zh, w2_other)
    wc += more

    loads[4].wait()
    loads[5].wait()
    for copy in h_copies:
        copy.wait_recv()
    for j in range(GROUPS):
        g_wide[j * CUT:(j + 1) * CUT, :] = h_dst[j].astype(jnp.float32)[0:CUT]
    average = g_wide[...] / GROUPS
    new_moment = outer_beta * mom_buf[...] + average
    mom_buf[...] = new_moment
    par_buf[...] = par_buf[...] - outer_rate * (average + outer_beta * new_moment)
    stores = [
        pltpu.make_async_copy(par_buf, params_out, store_sem.at[0]),
        pltpu.make_async_copy(mom_buf, moment_out, store_sem.at[1]),
    ]
    for copy in stores:
        copy.start()

    for copy in w3_own:
        copy.wait_recv()
    w_last = w_core(0, zh, 2)
    own_c = c_buf[0]

    def gi_block(j, k):
        blk = lax.dot_general(
            own_c, w_buf[(y + k) % 4, (x + j) % 4], (((1,), (1,)), ((), ())), preferred_element_type=jnp.float32
        )
        gi_buf[:, a_cols(j, k)] = blk.astype(jnp.bfloat16)
        copy = pltpu.make_async_copy(
            gi_buf.at[:, a_cols(j, k)], gi_out.at[:, a_cols(j, k)], store_sem.at[3 + 4 * j + k]
        )
        copy.start()
        stores.append(copy)

    for copy in wc:
        copy.wait_recv()
    for k in (0, 1, 3):
        for j in (0, 1, 3):
            gi_block(j, k)
    for copy in w3_other:
        copy.wait_recv()
    w_last += w_core(1, 1 - zh, 2)
    for copy in w_last:
        copy.wait_recv()
    for j in range(4):
        gi_block(j, 2)
    for k in (0, 1, 3):
        gi_block(2, k)

    swap.wait_recv()
    for copy in z_g:
        copy.wait_recv()
    gw_buf[:, mine] = total[rows(zh, c), :] + z_dst[0].astype(jnp.float32)
    others = pl.ds(pl.multiple_of((1 - c) * HALF, HALF), HALF)
    gw_buf[:, others] = swapped[...] + z_dst[1].astype(jnp.float32)
    stores.append(pltpu.make_async_copy(gw_buf, gw_out, store_sem.at[2]))
    stores[-1].start()

    for copy in sent:
        copy.wait_send()
    for j, k in A_ORDER:
        a_one(j, k).wait_send()
    for copy in stores:
        copy.wait()


def store(gi, gw, params, moment, gi_out, gw_out, params_out, moment_out, gi_buf, gw_buf, par_buf, mom_buf, sem):
    pieces = [
        (ref.at[pl.ds(i * 32, 32)], buf.at[pl.ds(i * 32, 32)], out.at[pl.ds(i * 32, 32)])
        for ref, buf, out in ((gi, gi_buf, gi_out),)
        for i in range(TOK // 32)
    ]
    pieces += [(gw, gw_buf, gw_out), (params, par_buf, params_out), (moment, mom_buf, moment_out)]
    loads = [pltpu.make_async_copy(p[0], p[1], sem.at[0, i]) for i, p in enumerate(pieces)]
    stores = [pltpu.make_async_copy(p[1], p[2], sem.at[1, i]) for i, p in enumerate(pieces)]
    for copy in loads:
        copy.start()
    for i in range(len(pieces)):
        loads[i].wait()
        stores[i].start()
    for copy in stores:
        copy.wait()


def body(activations, up_cotangent, up_weight, pseudo_grads, outer_params, outer_moment):
    bf16, f32 = jnp.bfloat16, jnp.float32
    dma = pltpu.SemaphoreType.DMA
    any_space = pl.BlockSpec(memory_space=pl.ANY)
    shapes = (((TOK, D), bf16), ((ROWS, FW), f32), ((ROWS, FRAG), f32), ((ROWS, FRAG), f32))
    results = pl.pallas_call(
        kernel,
        out_shape=tuple(jax.ShapeDtypeStruct(*shape) for shape in shapes),
        in_specs=[any_space] * 6,
        out_specs=(any_space,) * 4,
        scratch_shapes=[
            pltpu.VMEM((2 * TOK, D), bf16),
            pltpu.VMEM((2, TOK, FW), bf16),
            pltpu.VMEM((HALF, 2 * TOK), bf16),
            pltpu.VMEM((4, 4, PART, BLOCK), bf16),
            pltpu.VMEM((4, 4, PART, BLOCK), bf16),
            pltpu.VMEM((3, 2, 2, PART, BLOCK), bf16),
            pltpu.VMEM((3, 2, 2, PART, BLOCK), bf16),
            pltpu.VMEM((3, PART, BLOCK), bf16),
            pltpu.VMEM((3, PART, BLOCK), bf16),
            pltpu.VMEM((3, PART, BLOCK), bf16),
            pltpu.VMEM((3, PART, BLOCK), bf16),
            pltpu.VMEM((BLOCK, HALF), f32),
            pltpu.VMEM((2, ROWS, HALF), bf16),
            pltpu.VMEM((2, ROWS, HALF), bf16),
            pltpu.VMEM((ROWS, HALF), f32),
            pltpu.VMEM((ROWS, FW), f32),
            pltpu.VMEM((4, 4, BLOCK, FW), bf16),
            pltpu.VMEM((TOK, D), bf16),
            pltpu.VMEM((ROWS, FRAG), bf16),
            pltpu.VMEM((ROWS, FRAG), f32),
            pltpu.VMEM((GROUPS, PAD, FRAG), f32),
            pltpu.VMEM((GROUPS, PAD, FRAG), bf16),
            pltpu.VMEM((GROUPS, PAD, FRAG), bf16),
            pltpu.VMEM((GROUPS, PAD, FRAG), bf16),
            pltpu.VMEM((ROWS, FRAG), f32),
            pltpu.VMEM((ROWS, FRAG), f32),
            dma((6,)),
            dma((19,)),
            dma((2,)),
            dma((2,)),
            dma((4, 4)),
            dma((4, 4)),
            dma((2, 3, 2, 4)),
            dma((2, 3, 2, 4)),
            dma((2, 3, 2)),
            dma((2, 3, 2)),
            dma((4,)),
            dma((4,)),
            dma((2, 2, 3)),
            dma((2, 2, 3)),
            dma((2, 2, 2, 2, 4)),
            dma((2, 2, 2, 2, 4)),
            dma((2, 2, 4)),
            dma((2, 2, 4)),
            dma((GROUPS,)),
            dma((GROUPS,)),
            dma((GROUPS,)),
            dma((GROUPS,)),
        ],
        compiler_params=pltpu.CompilerParams(
            collective_id=0, has_side_effects=True, vmem_limit_bytes=62 * 1024 * 1024
        ),
        cost_estimate=pl.CostEstimate(flops=2 * 2 * TOK * D * FW, bytes_accessed=8 << 20, transcendentals=0),
        name="up_backward",
    )(
        activations[0], up_cotangent[0], up_weight[0], pseudo_grads[0], outer_params, outer_moment
    )
    gi, gw, new_params, new_moment = pl.pallas_call(
        store,
        out_shape=tuple(jax.ShapeDtypeStruct(*shape) for shape in shapes),
        in_specs=[any_space] * 4,
        out_specs=(any_space,) * 4,
        scratch_shapes=[pltpu.VMEM(*shape) for shape in shapes] + [dma((2, TOK // 32 + 3))],
        compiler_params=pltpu.CompilerParams(vmem_limit_bytes=62 * 1024 * 1024),
        name="store_results",
    )(*results)
    return gi[None], gw[None], new_params, new_moment


def solution(mesh):
    placed = (
        P("replica", "fsdp", None),
        P("replica", "fsdp", None),
        P("replica", "fsdp", None),
        P("replica", "fsdp", None),
        P("fsdp", None),
        P("fsdp", None),
    )
    return jax.shard_map(
        body,
        mesh=mesh,
        in_specs=placed,
        out_specs=(
            P("replica", "fsdp", None),
            P("replica", "fsdp", None),
            P("fsdp", None),
            P("fsdp", None),
        ),
        check_vma=False,
    )
```
